256 devices in a mesh: seq: 256 (over y, x, z, core).
Axes of the slice: x: 4, y: 4, z: 8, core: 2. Of those that a mesh axis runs over, the one named last changes fastest.
Arguments:
- queries: bfloat16 [256, 2, 256, 2048], P('seq'), may hold values from -12 to 12
- keys: bfloat16 [256, 2, 256, 512], P('seq'), may hold values from -4 to 4
- values: bfloat16 [256, 2, 256, 512], P('seq'), may hold values from -6 to 6
Outputs:
- attended: bfloat16 [256, 2, 256, 2048], P('seq')
The draws below stay inside these ranges and needn't reach their ends.
All inputs are finite; a program needn't handle non-finite values.
Results may differ from the reference program's by a relative error of at most 0.0034.
Values may be sent and summed in bfloat16 or wider, within the bound.
No kernel may reach another device: no remote copies, remote signals or barrier semaphores. Data moves between devices by JAX's collectives and lax.ppermute only.
A program may use at most 64 MiB of HBM per device.

```python
import jax
import jax.numpy as jnp
from jax import lax

HEADS = 32
KV_HEADS = 8
HEAD_DIM = 64
BLOCK = 256
BAND = 2
N_SEQ = 256


def draw_queries(key, part):
    key = jax.random.fold_in(key, 11)
    shape = (N_SEQ, 2, BLOCK, HEADS, HEAD_DIM)
    base = jnp.clip(2.0 * jax.random.normal(key, shape, jnp.float32), -8.0, 8.0)
    return base.reshape(N_SEQ, 2, BLOCK, HEADS * HEAD_DIM).astype(jnp.bfloat16)


def draw_keys(key, part):
    key = jax.random.fold_in(key, 23)
    shape = (N_SEQ, 2, BLOCK, KV_HEADS, HEAD_DIM)
    base = jnp.clip(jax.random.normal(key, shape, jnp.float32), -4.0, 4.0)
    return base.reshape(N_SEQ, 2, BLOCK, KV_HEADS * HEAD_DIM).astype(jnp.bfloat16)


def levels(rng, shape, cuts, least, high):
    gain = 1.0
    for axis_at, parts in cuts:
        steps = jax.random.uniform(jax.random.fold_in(jax.random.fold_in(rng, 6), axis_at), (parts,), jnp.float32, least / len(cuts), high / len(cuts))
        gain = gain * jnp.repeat(jnp.exp(steps), shape[axis_at] // parts).reshape((-1,) + (1,) * (len(shape) - 1 - axis_at))
    return gain


def bell_draw(rng, shape, deviation, bound, shards=(), held_as=jnp.bfloat16):
    gain = levels(rng, shape, shards, -0.22, 0.18) if shards else 1.0
    entries = jax.random.normal(rng, shape, jnp.float32) * deviation * gain
    return jnp.minimum(jnp.maximum(entries, -bound), bound).astype(held_as)


def setup_inputs(seed: int = 0) -> dict:
    arg_keys = jax.random.split(jax.random.key(seed), 4)
    return {
        "queries": draw_queries(jax.random.fold_in(arg_keys[3], 71), 0),
        "keys": draw_keys(jax.random.fold_in(arg_keys[3], 71), 0),
        "values": bell_draw(arg_keys[2], (N_SEQ, 2, BLOCK, KV_HEADS * HEAD_DIM), 1.0, 6.0, ((0, 256),)),
    }


def attend(query, key_rows, value_rows, valid):
    length = query.shape[0]
    per_group = HEADS // KV_HEADS
    inverse_root = 1.0 / (HEAD_DIM ** 0.5)

    def one_group(group_index):
        query_group = lax.dynamic_slice_in_dim(query, group_index * per_group * HEAD_DIM, per_group * HEAD_DIM, 1)
        query_group = query_group.reshape(length, per_group, HEAD_DIM).astype(jnp.float32)
        key_group = lax.dynamic_slice_in_dim(key_rows, group_index * HEAD_DIM, HEAD_DIM, 1).astype(jnp.float32)
        value_group = lax.dynamic_slice_in_dim(value_rows, group_index * HEAD_DIM, HEAD_DIM, 1).astype(jnp.float32)
        scores = jnp.einsum('qhd,kd->hqk', query_group, key_group) * inverse_root
        scores = jnp.where(valid[None], scores, jnp.float32(-1e30))
        peak = jnp.max(scores, axis=-1, keepdims=True)
        raw = jnp.exp(scores - peak)
        totals = jnp.sum(raw, axis=-1)
        weights = lax.optimization_barrier(raw.astype(jnp.bfloat16)).astype(jnp.float32)
        mixed = jnp.einsum('hqk,kd->qhd', weights, value_group) / totals.T[:, :, None]
        return mixed.reshape(length, per_group * HEAD_DIM)

    outputs = lax.map(one_group, jnp.arange(KV_HEADS, dtype=jnp.int32))
    return outputs.transpose(1, 0, 2).reshape(length, HEADS * HEAD_DIM).astype(jnp.bfloat16)


def band_mask(usable):
    causal = jnp.arange(BLOCK)[:, None] >= jnp.arange(BLOCK)[None, :]
    pieces = [jnp.broadcast_to(usable[offset], (BLOCK, BLOCK)) for offset in range(BAND, 0, -1)]
    return jnp.concatenate(pieces + [causal], axis=1)


def natural(tensor):
    return jnp.concatenate([tensor[:, 0], tensor[::-1, 1]], axis=0)


def reference(queries, keys, values):
    query_blocks = natural(queries)
    width = keys.shape[-1]
    filler = jnp.zeros((BAND, BLOCK, width), jnp.bfloat16)
    padded_keys = jnp.concatenate([filler, natural(keys)], axis=0)
    padded_values = jnp.concatenate([filler, natural(values)], axis=0)

    def per_block(block_index):
        query = lax.dynamic_index_in_dim(query_blocks, block_index, 0, keepdims=False)
        key_rows = lax.dynamic_slice_in_dim(padded_keys, block_index, BAND + 1, 0).reshape((BAND + 1) * BLOCK, width)
        value_rows = lax.dynamic_slice_in_dim(padded_values, block_index, BAND + 1, 0).reshape((BAND + 1) * BLOCK, width)
        usable = [block_index >= offset for offset in range(BAND + 1)]
        return attend(query, key_rows, value_rows, band_mask(usable))

    outputs = lax.map(per_block, jnp.arange(2 * N_SEQ, dtype=jnp.int32))
    return jnp.stack([outputs[:N_SEQ], outputs[N_SEQ:][::-1]], axis=1)
```

```python
import functools

import jax
import jax.numpy as jnp
from jax import lax
from jax.experimental import pallas as pl
from jax.experimental.pallas import tpu as pltpu
from jax.sharding import PartitionSpec as P

HEADS = 32
KV_HEADS = 8
HEAD_DIM = 64
BLOCK = 256
WIDTH = HEADS * HEAD_DIM
KV_WIDTH = KV_HEADS * HEAD_DIM
LANES = 128
F32 = jnp.float32
BF16 = jnp.bfloat16
NT = (((1,), (1,)), ((), ()))
NN = (((1,), (0,)), ((), ()))
SCALE = 1.0 / HEAD_DIM**0.5
TOTAL_LOW = 2.0**-80
TOTAL_HIGH = 2.0**100
MIB = 2**20


def low_lanes(rows):
    return lax.broadcasted_iota(jnp.int32, (rows, LANES), 1) < HEAD_DIM


def key_value_tiles(kv_ref, group, valid):
    column = LANES * (group // 2)
    keys = kv_ref[:, column : column + LANES] * BF16(SCALE)
    values = kv_ref[:, KV_WIDTH + column : KV_WIDTH + column + LANES]
    low = low_lanes(BLOCK)
    keep = low if group % 2 == 0 else ~low
    keys = jnp.where(keep, keys, BF16(0))
    values = jnp.where(keep, values, BF16(1))
    if valid is not None:
        keys, values = keys * valid, values * valid
    keys_other, values_other = pltpu.roll(keys, HEAD_DIM, 1), pltpu.roll(values, HEAD_DIM, 1)
    if group % 2 == 0:
        return (keys, keys_other), (values, values_other)
    return (keys_other, keys), (values_other, values)


def group_queries(q_ref, slot, group):
    column = 2 * LANES * group
    return jnp.concatenate(
        [q_ref[0, slot, :, column : column + LANES], q_ref[0, slot, :, column + LANES : column + 2 * LANES]],
        axis=0,
    )


def partial_sums(queries, kv_ref, group, diagonal=False, valid=None):
    keys, values = key_value_tiles(kv_ref, group, valid)
    rows = queries.shape[0]
    sums = []
    for parity in range(2):
        scores = lax.dot_general(queries, keys[parity], NT, preferred_element_type=F32)
        if diagonal:
            row = lax.broadcasted_iota(jnp.int32, (rows, BLOCK), 0) % BLOCK
            scores = jnp.where(row >= lax.broadcasted_iota(jnp.int32, (rows, BLOCK), 1), scores, -1e30)
        raw = jnp.exp(scores).astype(BF16)
        sums.append(lax.dot_general(raw, values[parity], NN, preferred_element_type=F32))
    return sums


def normalized(sums):
    low = low_lanes(sums[0].shape[0])
    total = pltpu.roll(jnp.where(low, sums[1], sums[0]), HEAD_DIM, 1)
    out = (jnp.where(low, sums[0], sums[1]) / total).astype(BF16)
    off = jnp.where((total > TOTAL_LOW) & (total < TOTAL_HIGH), 0.0, 1.0)
    return out, jnp.max(off, axis=0, keepdims=True)


def own_blocks(q_ref, x_ref, y_ref, acc_x, acc_y):
    parity = lax.axis_index("seq") % 2
    for group in range(KV_HEADS):
        for slot, kv_ref, acc in ((parity, x_ref, acc_x), (1 - parity, y_ref, acc_y)):
            sums = partial_sums(group_queries(q_ref, slot, group), kv_ref, group, diagonal=True)
            acc[group, 0], acc[group, 1] = sums


def add_near_y(q_ref, s_ref, acc_in, acc_out):
    slot = 1 - lax.axis_index("seq") % 2
    for group in range(KV_HEADS):
        sums = partial_sums(group_queries(q_ref, slot, group), s_ref, group)
        for parity in range(2):
            acc_out[group, parity] = acc_in[group, parity] + sums[parity]


def valid_from(first):
    return jnp.where(lax.axis_index("seq") == first, 0.0, 1.0).astype(BF16)


def finish_y(q_ref, b_ref, acc_in, out_ref, off_ref):
    slot = 1 - lax.axis_index("seq") % 2
    off = jnp.zeros((1, LANES), F32)
    for group in range(KV_HEADS):
        sums = partial_sums(group_queries(q_ref, slot, group), b_ref, group, valid=valid_from(1))
        out, bad = normalized([acc_in[group, parity] + sums[parity] for parity in range(2)])
        off = jnp.maximum(off, bad)
        for half in range(2):
            column = LANES * (2 * group + half)
            out_ref[:, column : column + LANES] = out[BLOCK * half : BLOCK * (half + 1)]
    off_ref[...] = jnp.broadcast_to(off, (8, LANES))


def add_near_x(q_ref, c_ref, acc_in, acc_out):
    slot = lax.axis_index("seq") % 2
    for group in range(KV_HEADS):
        sums = partial_sums(group_queries(q_ref, slot, group), c_ref, group, valid=valid_from(0))
        for parity in range(2):
            acc_out[group, parity] = acc_in[group, parity] + sums[parity]


def exact_block(q_ref, slot, blocks, usable, out_ref):
    low = low_lanes(BLOCK)
    causal = lax.broadcasted_iota(jnp.int32, (BLOCK, BLOCK), 0) >= lax.broadcasted_iota(
        jnp.int32, (BLOCK, BLOCK), 1
    )

    def slab(index, carry):
        kv_column = pl.multiple_of(LANES * (index // 4), LANES)
        column = pl.multiple_of(LANES * index, LANES)
        in_low = (index // 2) % 2 == 0
        queries = q_ref[0, slot, :, pl.ds(column, LANES)].astype(F32)
        outs = []
        for head in range(2):
            mine = low if head == 0 else ~low
            query = jnp.where(mine, queries, 0.0)
            shift_by = jnp.where(in_low, 0, HEAD_DIM)
            at_low = query if head == 0 else pltpu.roll(query, HEAD_DIM, 1)
            at_high = pltpu.roll(at_low, HEAD_DIM, 1)
            query = jnp.where(shift_by == 0, at_low, at_high).astype(BF16)
            scores = []
            for block, ok in zip(blocks, usable):
                keys = block[:, pl.ds(kv_column, LANES)]
                part = lax.dot_general(query, keys, NT, preferred_element_type=F32) * SCALE
                scores.append(jnp.where(causal if ok is None else ok, part, -1e30))
            peak = functools.reduce(jnp.maximum, [jnp.max(part, axis=1, keepdims=True) for part in scores])
            total, mixed = 0.0, 0.0
            for block, part in zip(blocks, scores):
                raw = jnp.exp(part - peak)
                total = total + jnp.sum(raw, axis=1, keepdims=True)
                values = block[:, pl.ds(pl.multiple_of(KV_WIDTH + kv_column, LANES), LANES)]
                mixed = mixed + lax.dot_general(raw.astype(BF16), values, NN, preferred_element_type=F32)
            mixed = mixed / total
            at_low = jnp.where(in_low, mixed, pltpu.roll(mixed, HEAD_DIM, 1))
            outs.append(at_low if head == 0 else pltpu.roll(at_low, HEAD_DIM, 1))
        out_ref[:, pl.ds(column, LANES)] = jnp.where(low, outs[0], outs[1]).astype(BF16)
        return carry

    lax.fori_loop(0, WIDTH // LANES, slab, 0)


def finish_x(
    q_ref, x_ref, y_ref, s_ref, b_ref, c_ref, a_ref, acc_in, y_done, y_off, out_ref, x_out, y_out, x_sems, y_sem
):
    index = lax.axis_index("seq")
    slot = index % 2
    y_copy = pltpu.make_async_copy(y_done, out_ref.at[0, 1 - slot], y_sem)
    y_copy.start()
    off = jnp.max(y_off[...], axis=0, keepdims=True)
    copies = []
    for group in range(KV_HEADS):
        sums = partial_sums(group_queries(q_ref, slot, group), a_ref, group, valid=valid_from(0))
        out, bad = normalized([acc_in[group, parity] + sums[parity] for parity in range(2)])
        off = jnp.maximum(off, bad)
        for half in range(2):
            column = LANES * (2 * group + half)
            x_out[:, column : column + LANES] = out[BLOCK * half : BLOCK * (half + 1)]
        if group % 2 == 1:
            columns = pl.ds(4 * LANES * (group // 2), 4 * LANES)
            copies.append(
                pltpu.make_async_copy(
                    x_out.at[:, columns], out_ref.at[0, slot, :, columns], x_sems.at[group // 2]
                )
            )
            copies[-1].start()
    for copy in copies:
        copy.wait()
    y_copy.wait()

    @pl.when(jnp.max(off) > 0.0)
    def _():
        exact_block(q_ref, slot, (x_ref, c_ref, a_ref), (None, index != 0, index != 0), x_out)
        exact_block(q_ref, 1 - slot, (y_ref, s_ref, b_ref), (None, index >= 0, index != 1), y_out)
        again = (
            pltpu.make_async_copy(x_out, out_ref.at[0, slot], x_sems.at[0]),
            pltpu.make_async_copy(y_out, out_ref.at[0, 1 - slot], y_sem),
        )
        for copy in again:
            copy.start()
        for copy in again:
            copy.wait()


ACC = jax.ShapeDtypeStruct((KV_HEADS, 2, 2 * BLOCK, LANES), F32)
ROWS = jax.ShapeDtypeStruct((BLOCK, WIDTH), BF16)
OFF = jax.ShapeDtypeStruct((8, LANES), F32)


def call(kernel, inputs, outputs, units, **more):
    vmem = pl.BlockSpec(memory_space=pltpu.VMEM)
    more.setdefault("out_specs", [vmem] * len(outputs))
    return pl.pallas_call(
        kernel,
        in_specs=[vmem] * inputs,
        out_shape=outputs,
        compiler_params=pltpu.CompilerParams(vmem_limit_bytes=24 * MIB),
        cost_estimate=pl.CostEstimate(
            flops=units * 10**10,
            bytes_accessed=1024,
            transcendentals=1024,
        ),
        **more,
    )


def on_device(queries, keys, values):
    count = lax.axis_size("seq")
    parity = lax.axis_index("seq") % 2
    both = jnp.concatenate([keys[0], values[0]], axis=-1)
    x = lax.dynamic_index_in_dim(both, parity, 0, keepdims=False)
    y = lax.dynamic_index_in_dim(both, 1 - parity, 0, keepdims=False)
    evens, odds = list(range(0, count, 2)), list(range(1, count, 2))
    ring = evens + odds[::-1]
    forth = list(zip(ring, ring[1:] + ring[:1]))
    ring = odds + evens[::-1]
    back = list(zip(ring, ring[1:] + ring[:1]))
    swap = [(i, i ^ 1) for i in range(count)]
    b = lax.ppermute(y, "seq", back)
    s = lax.ppermute(x, "seq", swap)
    acc_x, acc_y = call(own_blocks, 3, [ACC, ACC], 2)(queries, x, y)
    x_late, acc_x = lax.optimization_barrier((x, acc_x))
    a = lax.ppermute(x_late, "seq", forth)
    (acc_y,) = call(add_near_y, 3, [ACC], 1)(queries, s, acc_y)
    b, acc_y = lax.optimization_barrier((b, acc_y))
    c = lax.ppermute(b, "seq", swap)
    y_done, y_off = call(finish_y, 3, [ROWS, OFF], 1)(queries, b, acc_y)
    (acc_x,) = call(add_near_x, 3, [ACC], 1)(queries, c, acc_x)
    return call(
        finish_x,
        10,
        jax.ShapeDtypeStruct(queries.shape, BF16),
        1,
        out_specs=pl.BlockSpec(memory_space=pl.ANY),
        scratch_shapes=[
            pltpu.VMEM((BLOCK, WIDTH), BF16),
            pltpu.VMEM((BLOCK, WIDTH), BF16),
            pltpu.SemaphoreType.DMA((KV_HEADS // 2,)),
            pltpu.SemaphoreType.DMA,
        ],
    )(queries, x, y, s, b, c, a, acc_x, y_done, y_off)


def solution(mesh):
    placed = P("seq", None, None, None)
    return jax.shard_map(on_device, mesh=mesh, in_specs=(placed,) * 3, out_specs=placed, check_vma=False)
```

```python
import functools

import jax
import jax.numpy as jnp
from jax import lax
from jax.experimental import pallas as pl
from jax.experimental.pallas import tpu as pltpu
from jax.sharding import PartitionSpec as P

HEADS = 32
KV_HEADS = 8
HEAD_DIM = 64
BLOCK = 256
WIDTH = HEADS * HEAD_DIM
KV_WIDTH = KV_HEADS * HEAD_DIM
LANES = 128
F32 = jnp.float32
BF16 = jnp.bfloat16
NT = (((1,), (1,)), ((), ()))
NN = (((1,), (0,)), ((), ()))
SCALE = 1.0 / HEAD_DIM**0.5
TOTAL_LOW = 2.0**-80
TOTAL_HIGH = 2.0**100
MIB = 2**20
FLOPS = 10**10


def low_lanes(rows):
    return lax.broadcasted_iota(jnp.int32, (rows, LANES), 1) < HEAD_DIM


def key_value_tiles(kv_ref, group, valid):
    column = LANES * (group // 2)
    keys = kv_ref[:, column : column + LANES] * BF16(SCALE)
    values = kv_ref[:, KV_WIDTH + column : KV_WIDTH + column + LANES]
    low = low_lanes(BLOCK)
    keep = low if group % 2 == 0 else ~low
    keys = jnp.where(keep, keys, BF16(0))
    values = jnp.where(keep, values, BF16(1))
    if valid is not None:
        keys, values = keys * valid, values * valid
    keys_other, values_other = pltpu.roll(keys, HEAD_DIM, 1), pltpu.roll(values, HEAD_DIM, 1)
    if group % 2 == 0:
        return (keys, keys_other), (values, values_other)
    return (keys_other, keys), (values_other, values)


def group_queries(q_ref, slot, group):
    column = 2 * LANES * group
    return jnp.concatenate(
        [q_ref[0, slot, :, column : column + LANES], q_ref[0, slot, :, column + LANES : column + 2 * LANES]],
        axis=0,
    )


def partial_sums(queries, kv_refs, group, diagonal=False, valid=None):
    tiles = [key_value_tiles(kv_ref, group, valid) for kv_ref in kv_refs]
    rows = queries.shape[0]
    sums = []
    for parity in range(2):
        keys, values = (
            jnp.concatenate([tile[kind][parity] for tile in tiles], axis=0) for kind in range(2)
        )
        scores = lax.dot_general(queries, keys, NT, preferred_element_type=F32)
        if diagonal:
            row = lax.broadcasted_iota(jnp.int32, (rows, BLOCK), 0) % BLOCK
            causal = row >= lax.broadcasted_iota(jnp.int32, (rows, BLOCK), 1)
            own = jnp.where(causal, scores[:, :BLOCK], -1e30)
            scores = jnp.concatenate([own, scores[:, BLOCK:]], axis=1) if len(kv_refs) > 1 else own
        raw = jnp.exp(scores).astype(BF16)
        sums.append(lax.dot_general(raw, values, NN, preferred_element_type=F32))
    return sums


def normalized(sums):
    low = low_lanes(sums[0].shape[0])
    total = pltpu.roll(jnp.where(low, sums[1], sums[0]), HEAD_DIM, 1)
    out = (jnp.where(low, sums[0], sums[1]) / total).astype(BF16)
    off = jnp.where((total > TOTAL_LOW) & (total < TOTAL_HIGH), 0.0, 1.0)
    return out, jnp.max(off, axis=0, keepdims=True)


def start_x(q_ref, x_ref, acc):
    slot = lax.axis_index("seq") % 2
    for group in range(KV_HEADS):
        sums = partial_sums(group_queries(q_ref, slot, group), [x_ref], group, diagonal=True)
        acc[group, 0], acc[group, 1] = sums


def start_y(q_ref, y_ref, s_ref, acc):
    slot = 1 - lax.axis_index("seq") % 2
    for group in range(KV_HEADS):
        sums = partial_sums(group_queries(q_ref, slot, group), [y_ref, s_ref], group, diagonal=True)
        acc[group, 0], acc[group, 1] = sums


def valid_from(first):
    return jnp.where(lax.axis_index("seq") == first, 0.0, 1.0).astype(BF16)


def finish_y(q_ref, b_ref, acc_in, out_ref, off_ref):
    slot = 1 - lax.axis_index("seq") % 2
    off = jnp.zeros((1, LANES), F32)
    for group in range(KV_HEADS):
        sums = partial_sums(group_queries(q_ref, slot, group), [b_ref], group, valid=valid_from(1))
        out, bad = normalized([acc_in[group, parity] + sums[parity] for parity in range(2)])
        off = jnp.maximum(off, bad)
        for half in range(2):
            column = LANES * (2 * group + half)
            out_ref[:, column : column + LANES] = out[BLOCK * half : BLOCK * (half + 1)]
    off_ref[...] = jnp.broadcast_to(off, (8, LANES))


def add_near_x(q_ref, c_ref, acc_in, acc_out):
    slot = lax.axis_index("seq") % 2
    for group in range(KV_HEADS):
        sums = partial_sums(group_queries(q_ref, slot, group), [c_ref], group, valid=valid_from(0))
        for parity in range(2):
            acc_out[group, parity] = acc_in[group, parity] + sums[parity]


def exact_block(q_ref, slot, blocks, usable, out_ref):
    low = low_lanes(BLOCK)
    causal = lax.broadcasted_iota(jnp.int32, (BLOCK, BLOCK), 0) >= lax.broadcasted_iota(
        jnp.int32, (BLOCK, BLOCK), 1
    )

    def slab(index, carry):
        kv_column = pl.multiple_of(LANES * (index // 4), LANES)
        column = pl.multiple_of(LANES * index, LANES)
        in_low = (index // 2) % 2 == 0
        queries = q_ref[0, slot, :, pl.ds(column, LANES)].astype(F32)
        outs = []
        for head in range(2):
            mine = low if head == 0 else ~low
            query = jnp.where(mine, queries, 0.0)
            shift_by = jnp.where(in_low, 0, HEAD_DIM)
            at_low = query if head == 0 else pltpu.roll(query, HEAD_DIM, 1)
            at_high = pltpu.roll(at_low, HEAD_DIM, 1)
            query = jnp.where(shift_by == 0, at_low, at_high).astype(BF16)
            scores = []
            for block, ok in zip(blocks, usable):
                keys = block[:, pl.ds(kv_column, LANES)]
                part = lax.dot_general(query, keys, NT, preferred_element_type=F32) * SCALE
                scores.append(jnp.where(causal if ok is None else ok, part, -1e30))
            peak = functools.reduce(jnp.maximum, [jnp.max(part, axis=1, keepdims=True) for part in scores])
            total, mixed = 0.0, 0.0
            for block, part in zip(blocks, scores):
                raw = jnp.exp(part - peak)
                total = total + jnp.sum(raw, axis=1, keepdims=True)
                values = block[:, pl.ds(pl.multiple_of(KV_WIDTH + kv_column, LANES), LANES)]
                mixed = mixed + lax.dot_general(raw.astype(BF16), values, NN, preferred_element_type=F32)
            mixed = mixed / total
            at_low = jnp.where(in_low, mixed, pltpu.roll(mixed, HEAD_DIM, 1))
            outs.append(at_low if head == 0 else pltpu.roll(at_low, HEAD_DIM, 1))
        out_ref[:, pl.ds(column, LANES)] = jnp.where(low, outs[0], outs[1]).astype(BF16)
        return carry

    lax.fori_loop(0, WIDTH // LANES, slab, 0)


def finish_x(
    q_ref, x_ref, y_ref, s_ref, b_ref, c_ref, a_ref, acc_in, y_done, y_off, out_ref, x_out, y_out, x_sems, y_sem
):
    index = lax.axis_index("seq")
    slot = index % 2
    y_copy = pltpu.make_async_copy(y_done, out_ref.at[0, 1 - slot], y_sem)
    y_copy.start()
    off = jnp.max(y_off[...], axis=0, keepdims=True)
    copies = []
    for group in range(KV_HEADS):
        sums = partial_sums(group_queries(q_ref, slot, group), [a_ref], group, valid=valid_from(0))
        out, bad = normalized([acc_in[group, parity] + sums[parity] for parity in range(2)])
        off = jnp.maximum(off, bad)
        for half in range(2):
            column = LANES * (2 * group + half)
            x_out[:, column : column + LANES] = out[BLOCK * half : BLOCK * (half + 1)]
        if group % 2 == 1:
            columns = pl.ds(4 * LANES * (group // 2), 4 * LANES)
            copies.append(
                pltpu.make_async_copy(
                    x_out.at[:, columns], out_ref.at[0, slot, :, columns], x_sems.at[group // 2]
                )
            )
            copies[-1].start()
    for copy in copies:
        copy.wait()
    y_copy.wait()

    @pl.when(jnp.max(off) > 0.0)
    def _():
        exact_block(q_ref, slot, (x_ref, c_ref, a_ref), (None, index != 0, index != 0), x_out)
        exact_block(q_ref, 1 - slot, (y_ref, s_ref, b_ref), (None, index >= 0, index != 1), y_out)
        again = (
            pltpu.make_async_copy(x_out, out_ref.at[0, slot], x_sems.at[0]),
            pltpu.make_async_copy(y_out, out_ref.at[0, 1 - slot], y_sem),
        )
        for copy in again:
            copy.start()
        for copy in again:
            copy.wait()


ACC = jax.ShapeDtypeStruct((KV_HEADS, 2, 2 * BLOCK, LANES), F32)
ROWS = jax.ShapeDtypeStruct((BLOCK, WIDTH), BF16)
OFF = jax.ShapeDtypeStruct((8, LANES), F32)


def call(kernel, inputs, outputs, units, **more):
    vmem = pl.BlockSpec(memory_space=pltpu.VMEM)
    more.setdefault("out_specs", [vmem] * len(outputs))
    return pl.pallas_call(
        kernel,
        in_specs=[vmem] * inputs,
        out_shape=outputs,
        compiler_params=pltpu.CompilerParams(vmem_limit_bytes=24 * MIB),
        cost_estimate=pl.CostEstimate(
            flops=units * FLOPS,
            bytes_accessed=1024,
            transcendentals=1024,
        ),
        **more,
    )


def on_device(queries, keys, values):
    count = lax.axis_size("seq")
    parity = lax.axis_index("seq") % 2
    both = jnp.concatenate([keys[0], values[0]], axis=-1)
    x = lax.dynamic_index_in_dim(both, parity, 0, keepdims=False)
    y = lax.dynamic_index_in_dim(both, 1 - parity, 0, keepdims=False)
    evens, odds = list(range(0, count, 2)), list(range(1, count, 2))
    ring = evens + odds[::-1]
    forth = list(zip(ring, ring[1:] + ring[:1]))
    ring = odds + evens[::-1]
    back = list(zip(ring, ring[1:] + ring[:1]))
    swap = [(i, i ^ 1) for i in range(count)]
    b = lax.ppermute(y, "seq", back)
    s = lax.ppermute(x, "seq", swap)
    (acc_x,) = call(start_x, 2, [ACC], 1)(queries, x)
    x_late, acc_x = lax.optimization_barrier((x, acc_x))
    a = lax.ppermute(x_late, "seq", forth)
    (acc_y,) = call(start_y, 3, [ACC], 2)(queries, y, s)
    b, acc_y = lax.optimization_barrier((b, acc_y))
    c = lax.ppermute(b, "seq", swap)
    y_done, y_off = call(finish_y, 3, [ROWS, OFF], 1)(queries, b, acc_y)
    (acc_x,) = call(add_near_x, 3, [ACC], 1)(queries, c, acc_x)
    return call(
        finish_x,
        10,
        jax.ShapeDtypeStruct(queries.shape, BF16),
        1,
        out_specs=pl.BlockSpec(memory_space=pl.ANY),
        scratch_shapes=[
            pltpu.VMEM((BLOCK, WIDTH), BF16),
            pltpu.VMEM((BLOCK, WIDTH), BF16),
            pltpu.SemaphoreType.DMA((KV_HEADS // 2,)),
            pltpu.SemaphoreType.DMA,
        ],
    )(queries, x, y, s, b, c, a, acc_x, y_done, y_off)


def solution(mesh):
    placed = P("seq", None, None, None)
    return jax.shard_map(on_device, mesh=mesh, in_specs=(placed,) * 3, out_specs=placed, check_vma=False)
```

```python
import functools

import jax
import jax.numpy as jnp
from jax import lax
from jax.experimental import pallas as pl
from jax.experimental.pallas import tpu as pltpu
from jax.sharding import PartitionSpec as P

HEADS = 32
KV_HEADS = 8
HEAD_DIM = 64
BLOCK = 256
WIDTH = HEADS * HEAD_DIM
KV_WIDTH = KV_HEADS * HEAD_DIM
LANES = 128
F32 = jnp.float32
BF16 = jnp.bfloat16
NT = (((1,), (1,)), ((), ()))
NN = (((1,), (0,)), ((), ()))
SCALE = 1.0 / HEAD_DIM**0.5
TOTAL_LOW = 2.0**-80
TOTAL_HIGH = 2.0**100
MIB = 2**20
FLOPS = 10**10


def low_lanes(rows):
    return lax.broadcasted_iota(jnp.int32, (rows, LANES), 1) < HEAD_DIM


def key_value_tiles(kv_ref, group, valid):
    column = LANES * (group // 2)
    keys = kv_ref[:, column : column + LANES] * BF16(SCALE)
    values = kv_ref[:, KV_WIDTH + column : KV_WIDTH + column + LANES]
    low = low_lanes(BLOCK)
    keep = low if group % 2 == 0 else ~low
    keys = jnp.where(keep, keys, BF16(0))
    values = jnp.where(keep, values, BF16(1))
    if valid is not None:
        keys, values = keys * valid, values * valid
    keys_other, values_other = pltpu.roll(keys, HEAD_DIM, 1), pltpu.roll(values, HEAD_DIM, 1)
    if group % 2 == 0:
        return (keys, keys_other), (values, values_other)
    return (keys_other, keys), (values_other, values)


def group_queries(q_ref, slot, group):
    column = 2 * LANES * group
    return jnp.concatenate(
        [q_ref[0, slot, :, column : column + LANES], q_ref[0, slot, :, column + LANES : column + 2 * LANES]],
        axis=0,
    )


def partial_sums(queries, kv_refs, group, diagonal=False, valid=None):
    tiles = [key_value_tiles(kv_ref, group, valid) for kv_ref in kv_refs]
    rows = queries.shape[0]
    sums = []
    for parity in range(2):
        keys, values = (
            jnp.concatenate([tile[kind][parity] for tile in tiles], axis=0) for kind in range(2)
        )
        scores = lax.dot_general(queries, keys, NT, preferred_element_type=F32)
        if diagonal:
            row = lax.broadcasted_iota(jnp.int32, (rows, BLOCK), 0) % BLOCK
            causal = row >= lax.broadcasted_iota(jnp.int32, (rows, BLOCK), 1)
            own = jnp.where(causal, scores[:, :BLOCK], -1e30)
            scores = jnp.concatenate([own, scores[:, BLOCK:]], axis=1) if len(kv_refs) > 1 else own
        raw = jnp.exp(scores).astype(BF16)
        sums.append(lax.dot_general(raw, values, NN, preferred_element_type=F32))
    return sums


def normalized(sums):
    low = low_lanes(sums[0].shape[0])
    total = pltpu.roll(jnp.where(low, sums[1], sums[0]), HEAD_DIM, 1)
    out = (jnp.where(low, sums[0], sums[1]) / total).astype(BF16)
    off = jnp.where((total > TOTAL_LOW) & (total < TOTAL_HIGH), 0.0, 1.0)
    return out, jnp.max(off, axis=0, keepdims=True)


def start_x(q_ref, x_ref, acc):
    slot = lax.axis_index("seq") % 2
    for group in range(KV_HEADS):
        sums = partial_sums(group_queries(q_ref, slot, group), [x_ref], group, diagonal=True)
        acc[group, 0], acc[group, 1] = sums


def start_y(q_ref, y_ref, s_ref, acc):
    slot = 1 - lax.axis_index("seq") % 2
    for group in range(KV_HEADS):
        sums = partial_sums(group_queries(q_ref, slot, group), [y_ref, s_ref], group, diagonal=True)
        acc[group, 0], acc[group, 1] = sums


def valid_from(first):
    return jnp.where(lax.axis_index("seq") == first, 0.0, 1.0).astype(BF16)


def finish_y(q_ref, b_ref, acc_in, out_ref, off_ref):
    slot = 1 - lax.axis_index("seq") % 2
    off = jnp.zeros((1, LANES), F32)
    for group in range(KV_HEADS):
        sums = partial_sums(group_queries(q_ref, slot, group), [b_ref], group, valid=valid_from(1))
        out, bad = normalized([acc_in[group, parity] + sums[parity] for parity in range(2)])
        off = jnp.maximum(off, bad)
        for half in range(2):
            column = LANES * (2 * group + half)
            out_ref[:, column : column + LANES] = out[BLOCK * half : BLOCK * (half + 1)]
    off_ref[...] = jnp.broadcast_to(off, (8, LANES))


def add_near_x(q_ref, c_ref, acc_in, acc_out):
    slot = lax.axis_index("seq") % 2
    for group in range(KV_HEADS):
        sums = partial_sums(group_queries(q_ref, slot, group), [c_ref], group, valid=valid_from(0))
        for parity in range(2):
            acc_out[group, parity] = acc_in[group, parity] + sums[parity]


def exact_block(q_ref, slot, blocks, usable, out_ref):
    low = low_lanes(BLOCK)
    causal = lax.broadcasted_iota(jnp.int32, (BLOCK, BLOCK), 0) >= lax.broadcasted_iota(
        jnp.int32, (BLOCK, BLOCK), 1
    )

    def slab(index, carry):
        kv_column = pl.multiple_of(LANES * (index // 4), LANES)
        column = pl.multiple_of(LANES * index, LANES)
        in_low = (index // 2) % 2 == 0
        queries = q_ref[0, slot, :, pl.ds(column, LANES)].astype(F32)
        outs = []
        for head in range(2):
            mine = low if head == 0 else ~low
            query = jnp.where(mine, queries, 0.0)
            shift_by = jnp.where(in_low, 0, HEAD_DIM)
            at_low = query if head == 0 else pltpu.roll(query, HEAD_DIM, 1)
            at_high = pltpu.roll(at_low, HEAD_DIM, 1)
            query = jnp.where(shift_by == 0, at_low, at_high).astype(BF16)
            scores = []
            for block, ok in zip(blocks, usable):
                keys = block[:, pl.ds(kv_column, LANES)]
                part = lax.dot_general(query, keys, NT, preferred_element_type=F32) * SCALE
                scores.append(jnp.where(causal if ok is None else ok, part, -1e30))
            peak = functools.reduce(jnp.maximum, [jnp.max(part, axis=1, keepdims=True) for part in scores])
            total, mixed = 0.0, 0.0
            for block, part in zip(blocks, scores):
                raw = jnp.exp(part - peak)
                total = total + jnp.sum(raw, axis=1, keepdims=True)
                values = block[:, pl.ds(pl.multiple_of(KV_WIDTH + kv_column, LANES), LANES)]
                mixed = mixed + lax.dot_general(raw.astype(BF16), values, NN, preferred_element_type=F32)
            mixed = mixed / total
            at_low = jnp.where(in_low, mixed, pltpu.roll(mixed, HEAD_DIM, 1))
            outs.append(at_low if head == 0 else pltpu.roll(at_low, HEAD_DIM, 1))
        out_ref[:, pl.ds(column, LANES)] = jnp.where(low, outs[0], outs[1]).astype(BF16)
        return carry

    lax.fori_loop(0, WIDTH // LANES, slab, 0)


def finish_x(
    q_ref, x_ref, y_ref, s_ref, b_ref, c_ref, a_ref, acc_in, y_done, y_off, out_ref, x_out, y_out, x_sems, y_sem
):
    index = lax.axis_index("seq")
    slot = index % 2
    y_copy = pltpu.make_async_copy(y_done, out_ref.at[0, 1 - slot], y_sem)
    y_copy.start()
    off = jnp.max(y_off[...], axis=0, keepdims=True)
    copies = []
    for group in range(KV_HEADS):
        sums = partial_sums(group_queries(q_ref, slot, group), [a_ref], group, valid=valid_from(0))
        out, bad = normalized([acc_in[group, parity] + sums[parity] for parity in range(2)])
        off = jnp.maximum(off, bad)
        for half in range(2):
            column = LANES * (2 * group + half)
            x_out[:, column : column + LANES] = out[BLOCK * half : BLOCK * (half + 1)]
        columns = pl.ds(2 * LANES * group, 2 * LANES)
        copies.append(
            pltpu.make_async_copy(x_out.at[:, columns], out_ref.at[0, slot, :, columns], x_sems.at[group])
        )
        copies[-1].start()
    for copy in copies:
        copy.wait()
    y_copy.wait()

    @pl.when(jnp.max(off) > 0.0)
    def _():
        exact_block(q_ref, slot, (x_ref, c_ref, a_ref), (None, index != 0, index != 0), x_out)
        exact_block(q_ref, 1 - slot, (y_ref, s_ref, b_ref), (None, index >= 0, index != 1), y_out)
        again = (
            pltpu.make_async_copy(x_out, out_ref.at[0, slot], x_sems.at[0]),
            pltpu.make_async_copy(y_out, out_ref.at[0, 1 - slot], y_sem),
        )
        for copy in again:
            copy.start()
        for copy in again:
            copy.wait()


ACC = jax.ShapeDtypeStruct((KV_HEADS, 2, 2 * BLOCK, LANES), F32)
ROWS = jax.ShapeDtypeStruct((BLOCK, WIDTH), BF16)
OFF = jax.ShapeDtypeStruct((8, LANES), F32)


def call(kernel, inputs, outputs, units, **more):
    vmem = pl.BlockSpec(memory_space=pltpu.VMEM)
    more.setdefault("out_specs", [vmem] * len(outputs))
    return pl.pallas_call(
        kernel,
        in_specs=[vmem] * inputs,
        out_shape=outputs,
        compiler_params=pltpu.CompilerParams(vmem_limit_bytes=24 * MIB),
        cost_estimate=pl.CostEstimate(
            flops=units * FLOPS,
            bytes_accessed=1024,
            transcendentals=1024,
        ),
        **more,
    )


def on_device(queries, keys, values):
    count = lax.axis_size("seq")
    parity = lax.axis_index("seq") % 2
    both = jnp.concatenate([keys[0], values[0]], axis=-1)
    x = lax.dynamic_index_in_dim(both, parity, 0, keepdims=False)
    y = lax.dynamic_index_in_dim(both, 1 - parity, 0, keepdims=False)
    evens, odds = list(range(0, count, 2)), list(range(1, count, 2))
    ring = evens + odds[::-1]
    forth = list(zip(ring, ring[1:] + ring[:1]))
    ring = odds + evens[::-1]
    back = list(zip(ring, ring[1:] + ring[:1]))
    swap = [(i, i ^ 1) for i in range(count)]
    b = lax.ppermute(y, "seq", back)
    s = lax.ppermute(x, "seq", swap)
    (acc_x,) = call(start_x, 2, [ACC], 1)(queries, x)
    x_late, acc_x = lax.optimization_barrier((x, acc_x))
    a = lax.ppermute(x_late, "seq", forth)
    queries, acc_x, y = lax.optimization_barrier((queries, acc_x, y))
    (acc_y,) = call(start_y, 3, [ACC], 2)(queries, y, s)
    b, acc_y = lax.optimization_barrier((b, acc_y))
    c = lax.ppermute(b, "seq", swap)
    y_done, y_off = call(finish_y, 3, [ROWS, OFF], 1)(queries, b, acc_y)
    (acc_x,) = call(add_near_x, 3, [ACC], 1)(queries, c, acc_x)
    return call(
        finish_x,
        10,
        jax.ShapeDtypeStruct(queries.shape, BF16),
        1,
        out_specs=pl.BlockSpec(memory_space=pl.ANY),
        scratch_shapes=[
            pltpu.VMEM((BLOCK, WIDTH), BF16),
            pltpu.VMEM((BLOCK, WIDTH), BF16),
            pltpu.SemaphoreType.DMA((KV_HEADS,)),
            pltpu.SemaphoreType.DMA,
        ],
    )(queries, x, y, s, b, c, a, acc_x, y_done, y_off)


def solution(mesh):
    placed = P("seq", None, None, None)
    return jax.shard_map(on_device, mesh=mesh, in_specs=(placed,) * 3, out_specs=placed, check_vma=False)
```

```python
import functools

import jax
import jax.numpy as jnp
from jax import lax
from jax.experimental import pallas as pl
from jax.experimental.pallas import tpu as pltpu
from jax.sharding import PartitionSpec as P

HEADS = 32
KV_HEADS = 8
HEAD_DIM = 64
BLOCK = 256
WIDTH = HEADS * HEAD_DIM
KV_WIDTH = KV_HEADS * HEAD_DIM
LANES = 128
F32 = jnp.float32
BF16 = jnp.bfloat16
NT = (((1,), (1,)), ((), ()))
NN = (((1,), (0,)), ((), ()))
SCALE = 1.0 / HEAD_DIM**0.5
TOTAL_LOW = 2.0**-80
TOTAL_HIGH = 2.0**100
MIB = 2**20
RUN = 16
FLOPS = 10**10


def low_lanes(rows):
    return lax.broadcasted_iota(jnp.int32, (rows, LANES), 1) < HEAD_DIM


def key_value_tiles(kv_ref, group, valid):
    column = LANES * (group // 2)
    keys = kv_ref[:, column : column + LANES] * BF16(SCALE)
    values = kv_ref[:, KV_WIDTH + column : KV_WIDTH + column + LANES]
    low = low_lanes(BLOCK)
    keep = low if group % 2 == 0 else ~low
    keys = jnp.where(keep, keys, BF16(0))
    values = jnp.where(keep, values, BF16(1))
    if valid is not None:
        keys, values = keys * valid, values * valid
    keys_other, values_other = pltpu.roll(keys, HEAD_DIM, 1), pltpu.roll(values, HEAD_DIM, 1)
    if group % 2 == 0:
        return (keys, keys_other), (values, values_other)
    return (keys_other, keys), (values_other, values)


def group_queries(q_ref, slot, group):
    column = 2 * LANES * group
    return jnp.concatenate(
        [q_ref[0, slot, :, column : column + LANES], q_ref[0, slot, :, column + LANES : column + 2 * LANES]],
        axis=0,
    )


def partial_sums(queries, kv_refs, group, diagonal=False, valid=None):
    tiles = [key_value_tiles(kv_ref, group, valid) for kv_ref in kv_refs]
    rows = queries.shape[0]
    sums = []
    for parity in range(2):
        keys, values = (
            jnp.concatenate([tile[kind][parity] for tile in tiles], axis=0) for kind in range(2)
        )
        scores = lax.dot_general(queries, keys, NT, preferred_element_type=F32)
        if diagonal:
            row = lax.broadcasted_iota(jnp.int32, (rows, BLOCK), 0) % BLOCK
            causal = row >= lax.broadcasted_iota(jnp.int32, (rows, BLOCK), 1)
            own = jnp.where(causal, scores[:, :BLOCK], -1e30)
            scores = jnp.concatenate([own, scores[:, BLOCK:]], axis=1) if len(kv_refs) > 1 else own
        raw = jnp.exp(scores).astype(BF16)
        sums.append(lax.dot_general(raw, values, NN, preferred_element_type=F32))
    return sums


def normalized(sums):
    low = low_lanes(sums[0].shape[0])
    total = pltpu.roll(jnp.where(low, sums[1], sums[0]), HEAD_DIM, 1)
    out = (jnp.where(low, sums[0], sums[1]) / total).astype(BF16)
    off = jnp.where((total > TOTAL_LOW) & (total < TOTAL_HIGH), 0.0, 1.0)
    return out, jnp.max(off, axis=0, keepdims=True)


def in_early_chip():
    index = lax.axis_index("seq")
    return (index % RUN < 2) & (index >= RUN)


def early_and_odd():
    index = lax.axis_index("seq")
    return (index % RUN == 1) & (index >= RUN)


def start_x(q_ref, x_ref, acc):
    slot = lax.axis_index("seq") % 2
    for group in range(KV_HEADS):
        sums = partial_sums(group_queries(q_ref, slot, group), [x_ref], group, diagonal=True)
        acc[group, 0], acc[group, 1] = sums


def start_y(q_ref, kv_refs, acc):
    slot = 1 - lax.axis_index("seq") % 2
    for group in range(KV_HEADS):
        sums = partial_sums(group_queries(q_ref, slot, group), kv_refs, group, diagonal=True)
        acc[group, 0], acc[group, 1] = sums


def start_early(q_ref, x_ref, acc_x):
    @pl.when(in_early_chip())
    def _():
        start_x(q_ref, x_ref, acc_x)


def start_late(q_ref, x_ref, y_ref, acc_x_in, acc_x, acc_y):
    @pl.when(~in_early_chip())
    def _():
        start_x(q_ref, x_ref, acc_x)

    @pl.when(early_and_odd())
    def _():
        start_y(q_ref, [y_ref], acc_y)


def near_y(q_ref, y_ref, s_ref, acc_in, acc):
    @pl.when(~early_and_odd())
    def _():
        start_y(q_ref, [y_ref, s_ref], acc)

    @pl.when(early_and_odd())
    def _():
        slot = 1 - lax.axis_index("seq") % 2
        for group in range(KV_HEADS):
            sums = partial_sums(group_queries(q_ref, slot, group), [s_ref], group)
            for parity in range(2):
                acc[group, parity] = acc_in[group, parity] + sums[parity]


def valid_from(first):
    return jnp.where(lax.axis_index("seq") == first, 0.0, 1.0).astype(BF16)


def finish_y(q_ref, b_ref, acc_in, out_ref, off_ref):
    slot = 1 - lax.axis_index("seq") % 2
    off = jnp.zeros((1, LANES), F32)
    for group in range(KV_HEADS):
        sums = partial_sums(group_queries(q_ref, slot, group), [b_ref], group, valid=valid_from(1))
        out, bad = normalized([acc_in[group, parity] + sums[parity] for parity in range(2)])
        off = jnp.maximum(off, bad)
        for half in range(2):
            column = LANES * (2 * group + half)
            out_ref[:, column : column + LANES] = out[BLOCK * half : BLOCK * (half + 1)]
    off_ref[...] = jnp.broadcast_to(off, (8, LANES))


def add_near_x(q_ref, c_ref, acc_in, acc_out):
    slot = lax.axis_index("seq") % 2
    for group in range(KV_HEADS):
        sums = partial_sums(group_queries(q_ref, slot, group), [c_ref], group, valid=valid_from(0))
        for parity in range(2):
            acc_out[group, parity] = acc_in[group, parity] + sums[parity]


def exact_block(q_ref, slot, blocks, usable, out_ref):
    low = low_lanes(BLOCK)
    causal = lax.broadcasted_iota(jnp.int32, (BLOCK, BLOCK), 0) >= lax.broadcasted_iota(
        jnp.int32, (BLOCK, BLOCK), 1
    )

    def slab(index, carry):
        kv_column = pl.multiple_of(LANES * (index // 4), LANES)
        column = pl.multiple_of(LANES * index, LANES)
        in_low = (index // 2) % 2 == 0
        queries = q_ref[0, slot, :, pl.ds(column, LANES)].astype(F32)
        outs = []
        for head in range(2):
            mine = low if head == 0 else ~low
            query = jnp.where(mine, queries, 0.0)
            shift_by = jnp.where(in_low, 0, HEAD_DIM)
            at_low = query if head == 0 else pltpu.roll(query, HEAD_DIM, 1)
            at_high = pltpu.roll(at_low, HEAD_DIM, 1)
            query = jnp.where(shift_by == 0, at_low, at_high).astype(BF16)
            scores = []
            for block, ok in zip(blocks, usable):
                keys = block[:, pl.ds(kv_column, LANES)]
                part = lax.dot_general(query, keys, NT, preferred_element_type=F32) * SCALE
                scores.append(jnp.where(causal if ok is None else ok, part, -1e30))
            peak = functools.reduce(jnp.maximum, [jnp.max(part, axis=1, keepdims=True) for part in scores])
            total, mixed = 0.0, 0.0
            for block, part in zip(blocks, scores):
                raw = jnp.exp(part - peak)
                total = total + jnp.sum(raw, axis=1, keepdims=True)
                values = block[:, pl.ds(pl.multiple_of(KV_WIDTH + kv_column, LANES), LANES)]
                mixed = mixed + lax.dot_general(raw.astype(BF16), values, NN, preferred_element_type=F32)
            mixed = mixed / total
            at_low = jnp.where(in_low, mixed, pltpu.roll(mixed, HEAD_DIM, 1))
            outs.append(at_low if head == 0 else pltpu.roll(at_low, HEAD_DIM, 1))
        out_ref[:, pl.ds(column, LANES)] = jnp.where(low, outs[0], outs[1]).astype(BF16)
        return carry

    lax.fori_loop(0, WIDTH // LANES, slab, 0)


def finish_x(
    q_ref, x_ref, y_ref, s_ref, b_ref, c_ref, a_ref, acc_in, y_done, y_off, out_ref, x_out, y_out, x_sems, y_sem
):
    index = lax.axis_index("seq")
    slot = index % 2
    y_copy = pltpu.make_async_copy(y_done, out_ref.at[0, 1 - slot], y_sem)
    y_copy.start()
    off = jnp.max(y_off[...], axis=0, keepdims=True)
    copies = []
    for group in range(KV_HEADS):
        sums = partial_sums(group_queries(q_ref, slot, group), [a_ref], group, valid=valid_from(0))
        out, bad = normalized([acc_in[group, parity] + sums[parity] for parity in range(2)])
        off = jnp.maximum(off, bad)
        for half in range(2):
            column = LANES * (2 * group + half)
            x_out[:, column : column + LANES] = out[BLOCK * half : BLOCK * (half + 1)]
        if group % 2 == 1:
            columns = pl.ds(4 * LANES * (group // 2), 4 * LANES)
            copies.append(
                pltpu.make_async_copy(
                    x_out.at[:, columns], out_ref.at[0, slot, :, columns], x_sems.at[group // 2]
                )
            )
            copies[-1].start()
    for copy in copies:
        copy.wait()
    y_copy.wait()

    @pl.when(jnp.max(off) > 0.0)
    def _():
        exact_block(q_ref, slot, (x_ref, c_ref, a_ref), (None, index != 0, index != 0), x_out)
        exact_block(q_ref, 1 - slot, (y_ref, s_ref, b_ref), (None, index >= 0, index != 1), y_out)
        again = (
            pltpu.make_async_copy(x_out, out_ref.at[0, slot], x_sems.at[0]),
            pltpu.make_async_copy(y_out, out_ref.at[0, 1 - slot], y_sem),
        )
        for copy in again:
            copy.start()
        for copy in again:
            copy.wait()


ACC = jax.ShapeDtypeStruct((KV_HEADS, 2, 2 * BLOCK, LANES), F32)
ROWS = jax.ShapeDtypeStruct((BLOCK, WIDTH), BF16)
OFF = jax.ShapeDtypeStruct((8, LANES), F32)


def call(kernel, inputs, outputs, units, **more):
    vmem = pl.BlockSpec(memory_space=pltpu.VMEM)
    more.setdefault("out_specs", [vmem] * len(outputs))
    return pl.pallas_call(
        kernel,
        in_specs=[vmem] * inputs,
        out_shape=outputs,
        compiler_params=pltpu.CompilerParams(vmem_limit_bytes=24 * MIB),
        cost_estimate=pl.CostEstimate(
            flops=units * FLOPS,
            bytes_accessed=1024,
            transcendentals=1024,
        ),
        **more,
    )


def on_device(queries, keys, values):
    count = lax.axis_size("seq")
    parity = lax.axis_index("seq") % 2
    both = jnp.concatenate([keys[0], values[0]], axis=-1)
    x = lax.dynamic_index_in_dim(both, parity, 0, keepdims=False)
    y = lax.dynamic_index_in_dim(both, 1 - parity, 0, keepdims=False)
    evens, odds = list(range(0, count, 2)), list(range(1, count, 2))
    ring = evens + odds[::-1]
    forth = list(zip(ring, ring[1:] + ring[:1]))
    ring = odds + evens[::-1]
    back = list(zip(ring, ring[1:] + ring[:1]))
    swap = [(i, i ^ 1) for i in range(count)]
    s = lax.ppermute(x, "seq", swap)
    (acc_x,) = call(start_early, 2, [ACC], 1)(queries, x)
    y_late, acc_x = lax.optimization_barrier((y, acc_x))
    b = lax.ppermute(y_late, "seq", back)
    acc_x, acc_y = call(start_late, 4, [ACC, ACC], 1, input_output_aliases={3: 0})(queries, x, y, acc_x)
    x_late, acc_x = lax.optimization_barrier((x, acc_x))
    a = lax.ppermute(x_late, "seq", forth)
    (acc_y,) = call(near_y, 4, [ACC], 2, input_output_aliases={3: 0})(queries, y, s, acc_y)
    b, acc_y = lax.optimization_barrier((b, acc_y))
    c = lax.ppermute(b, "seq", swap)
    y_done, y_off = call(finish_y, 3, [ROWS, OFF], 1)(queries, b, acc_y)
    (acc_x,) = call(add_near_x, 3, [ACC], 1)(queries, c, acc_x)
    return call(
        finish_x,
        10,
        jax.ShapeDtypeStruct(queries.shape, BF16),
        1,
        out_specs=pl.BlockSpec(memory_space=pl.ANY),
        scratch_shapes=[
            pltpu.VMEM((BLOCK, WIDTH), BF16),
            pltpu.VMEM((BLOCK, WIDTH), BF16),
            pltpu.SemaphoreType.DMA((KV_HEADS // 2,)),
            pltpu.SemaphoreType.DMA,
        ],
    )(queries, x, y, s, b, c, a, acc_x, y_done, y_off)


def solution(mesh):
    placed = P("seq", None, None, None)
    return jax.shard_map(on_device, mesh=mesh, in_specs=(placed,) * 3, out_specs=placed, check_vma=False)
```
